32 devices in a mesh: seq: 16 (over z, x, core), fsdp: 2 (over y).
Axes of the slice: x: 2, y: 2, z: 4, core: 2. Of those that a mesh axis runs over, the one named last changes fastest.
Arguments:
- queries: bfloat16 [2, 2048, 2048], P('fsdp', 'seq'), may hold values from -6 to 6
- key_vectors: bfloat16 [2, 2048, 2048], P('fsdp', 'seq'), may hold values from -6 to 6
- value_vectors: bfloat16 [2, 2048, 2048], P('fsdp', 'seq'), may hold values from -6 to 6
- out_grad: bfloat16 [2, 2048, 2048], P('fsdp', 'seq'), may hold values from -6 to 6
- out_weight: bfloat16 [2048, 2048], P(None, 'fsdp'), may hold values from -0.125 to 0.125
Outputs:
- query_grad: bfloat16 [2, 2048, 2048], P('fsdp', 'seq')
- key_grad: bfloat16 [2, 2048, 2048], P('fsdp', 'seq')
- value_grad: bfloat16 [2, 2048, 2048], P('fsdp', 'seq')
- weight_grad: float32 [2048, 2048], P('seq', 'fsdp')
The draws below stay inside these ranges and needn't reach their ends.
All inputs are finite; a program needn't handle non-finite values.
Results may differ from the reference program's by a relative error of at most 0.005.
Values may be sent and summed in bfloat16 or wider, within the bound.
No kernel may reach another device: no remote copies, remote signals or barrier semaphores. Data moves between devices by JAX's collectives and lax.ppermute only.
A program may use at most 192 MiB of HBM per device.

```python
import math
import jax
import jax.numpy as jnp
from jax import lax

D = 2048
HEADS = 16
HEAD_DIM = 128
BLOCK = 128
HD = 2048
LENGTH = 2048
SEQS = 2


def spiked(values, key, source, target, blocks, factor):
    def block_of(position):
        return (jnp.arange(values.shape[position]) // (values.shape[position] // blocks)).reshape((-1,) + (1,) * (values.ndim - 1 - position))

    near = jax.random.permutation(key, blocks)[block_of(target)]
    second = (block_of(target) + blocks // 2) % blocks
    return jnp.where((block_of(source) == near) | (block_of(source) == second), factor * values, values)


def shard_levels(stream_key, extent, shards, smallest, largest):
    def one(axis_at, parts):
        heights = jax.random.uniform(jax.random.fold_in(jax.random.fold_in(stream_key, 6), axis_at), (parts,), jnp.float32, smallest / len(shards), largest / len(shards))
        return jnp.repeat(jnp.exp(heights), extent[axis_at] // parts).reshape((-1,) + (1,) * (len(extent) - axis_at - 1))

    level = one(*shards[0])
    for cut in shards[1:]:
        level = level * one(*cut)
    return level


def centred(rng, shape, deviation, bound, cuts=(), dtype=jnp.bfloat16):
    array = jax.random.normal(rng, shape, jnp.float32) * deviation
    if len(cuts) > 0:
        array = shard_levels(rng, shape, cuts, -0.22, 0.18) * array
    return jnp.clip(array, min=-bound, max=bound).astype(dtype)


def bell_draw_with(stream_key, dims, deviation, bound, cuts, heavy, dtype=jnp.bfloat16):
    values = deviation * jax.random.normal(stream_key, dims, jnp.float32)
    if cuts:
        values = values * shard_levels(stream_key, dims, cuts, -0.22, 0.18)
    return jnp.clip(spiked(values, jax.random.fold_in(stream_key, 3), *heavy), -bound, bound).astype(dtype)


def setup_inputs(seed: int = 0) -> dict:
    keys = jax.random.split(jax.random.key(seed), 6)
    return {
        "queries": centred(keys[0], (SEQS, LENGTH, HD), 1.0, 6.0, ((0, 2), (1, 16))),
        "key_vectors": centred(keys[1], (SEQS, LENGTH, HD), 1.0, 6.0, ((0, 2), (1, 16))),
        "value_vectors": centred(keys[2], (SEQS, LENGTH, HD), 1.0, 6.0, ((0, 2), (1, 16))),
        "out_grad": bell_draw_with(keys[3], (SEQS, LENGTH, D), 1.0, 6.0, ((0, 2), (1, 16)), (1, 2, 16, 2.0)),
        "out_weight": centred(keys[4], (D, HD), HD ** -0.5, 0.125, ((1, 2),)),
    }


def to_low(values_in):
    return lax.optimization_barrier(values_in.astype(jnp.bfloat16)).astype(jnp.float32)

def block_terms(queries, key_vectors, value_vectors, grads, factor):
    length = queries.shape[0]
    blocks = length // BLOCK
    shape_four = (blocks, BLOCK, HEADS, HEAD_DIM)
    query_wide = queries.reshape(shape_four)
    keys_wide = key_vectors.reshape(shape_four)
    values_wide = value_vectors.reshape(shape_four)
    grads_wide = grads.reshape(shape_four)
    highest = lax.Precision.HIGHEST
    key_value = jnp.einsum('nshd,nshe->nhde', keys_wide, values_wide, precision=highest)
    query_cot = jnp.einsum('nthd,nthe->nhde', query_wide, grads_wide, precision=highest)
    s_before = jnp.cumsum(key_value, 0) - key_value
    g_after = lax.optimization_barrier(jnp.sum(query_cot, 0)) - jnp.cumsum(query_cot, 0)
    causal = jnp.tril(jnp.ones((BLOCK, BLOCK), jnp.float32))
    scores = jnp.einsum('nthd,nshd->nhts', query_wide, keys_wide, precision=highest) * causal
    mixing = jnp.einsum('nthe,nshe->nhts', grads_wide, values_wide, precision=highest) * causal
    scores = to_low(scores)
    mixing = to_low(mixing)
    attended = jnp.einsum('nthd,nhde->nthe', query_wide, s_before, precision=highest)
    attended = attended + jnp.einsum('nhts,nshe->nthe', scores, values_wide, precision=highest)
    query_grad = jnp.einsum('nthe,nhde->nthd', grads_wide, s_before, precision=highest)
    query_grad = query_grad + jnp.einsum('nhts,nshd->nthd', mixing, keys_wide, precision=highest)
    key_grad = jnp.einsum('nshe,nhde->nshd', values_wide, g_after, precision=highest)
    key_grad = key_grad + jnp.einsum('nhts,nthd->nshd', mixing, query_wide, precision=highest)
    value_grad = jnp.einsum('nshd,nhde->nshe', keys_wide, g_after, precision=highest)
    value_grad = value_grad + jnp.einsum('nhts,nthe->nshe', scores, grads_wide, precision=highest)
    flat = (length, HEADS * HEAD_DIM)
    return (factor * attended.reshape(flat), factor * query_grad.reshape(flat), factor * key_grad.reshape(flat), factor * value_grad.reshape(flat))

def reference(queries, key_vectors, value_vectors, out_grad, out_weight):
    seq_count, length, all_width = queries.shape
    grad_rows = out_grad.reshape(seq_count * length, D)
    grad_attn = jnp.dot(grad_rows, out_weight, preferred_element_type=jnp.float32)
    grad_attn = grad_attn.astype(jnp.bfloat16).reshape(seq_count, length, all_width)
    factor = 1.0 / math.sqrt(HEAD_DIM * length)

    def one_sequence(items):
        attended, query_grad, key_grad, value_grad = block_terms(items[0].astype(jnp.float32), items[1].astype(jnp.float32), items[2].astype(jnp.float32), items[3].astype(jnp.float32), factor)
        return (attended.astype(jnp.bfloat16), query_grad.astype(jnp.bfloat16), key_grad.astype(jnp.bfloat16), value_grad.astype(jnp.bfloat16))
    results = lax.map(one_sequence, (queries, key_vectors, value_vectors, grad_attn))
    attended = results[0].reshape(seq_count * length, all_width)
    weight_grad = lax.dot_general(grad_rows, attended, (((0,), (0,)), ((), ())), preferred_element_type=jnp.float32)
    weight_grad = weight_grad * (1.0 / math.sqrt(seq_count * length))
    return (results[1], results[2], results[3], weight_grad)
```

```python
import math

import jax
import jax.numpy as jnp
from jax import lax
from jax.experimental import pallas as pl
from jax.experimental.pallas import tpu as pltpu
from jax.sharding import PartitionSpec as P

HEADS = 16
HEAD_DIM = 128
BLOCK = 128
PLANE = 4
SLOTS = HEADS // PLANE
F32 = jnp.float32
BF16 = jnp.bfloat16
VMEM_LIMIT = 40 * 1024 * 1024


def dot(a, b, contract_a, contract_b):
    dims = (((contract_a,), (contract_b,)), ((), ()))
    return lax.dot_general(a, b, dims, preferred_element_type=F32)


def call(kernel, ids, arrays, outs):
    vmem = pl.BlockSpec(memory_space=pltpu.VMEM)
    return pl.pallas_call(
        kernel,
        out_shape=[jax.ShapeDtypeStruct(shape, dtype) for shape, dtype in outs],
        in_specs=[pl.BlockSpec(memory_space=pltpu.SMEM)] + [vmem] * len(arrays),
        out_specs=[vmem] * len(outs),
        compiler_params=pltpu.CompilerParams(vmem_limit_bytes=VMEM_LIMIT),
    )(ids, *arrays)


def columns(head):
    return pl.ds(pl.multiple_of(head * HEAD_DIM, HEAD_DIM), HEAD_DIM)


def state_kernel(ids, a_ref, b_ref, mine_ref, send_ref):
    x, c = (ids[1], ids[2])
    for other, out in ((0, mine_ref), (1, send_ref)):
        for far in range(2):
            for slot in range(SLOTS):
                head = 4 * slot + 2 * (x ^ far) + (c ^ other)
                state = dot(a_ref[0, :, columns(head)], b_ref[0, :, columns(head)], 0, 0)
                out[far, slot] = state.astype(out.dtype)


def grad_state_kernel(pieces, ids, a_ref, *refs):
    f = ids[3]
    whole_ref, mine_ref, send_ref = refs[pieces:]
    width = refs[0].shape[1]
    for r in range(pieces):
        at = lax.rem(f + r, pieces) * width
        whole_ref[0, :, pl.ds(pl.multiple_of(at, HEAD_DIM), width)] = refs[r][...]
    state_kernel(ids, a_ref, whole_ref, mine_ref, send_ref)


def masked(scores):
    rows = lax.broadcasted_iota(jnp.int32, (BLOCK, BLOCK), 0)
    cols = lax.broadcasted_iota(jnp.int32, (BLOCK, BLOCK), 1)
    return jnp.where(rows >= cols, scores, 0.0).astype(BF16)


def each_head(ids, body):
    x, c = (ids[1], ids[2])
    for other in range(2):
        for far in range(2):
            for slot in range(SLOTS):
                head = 4 * slot + 2 * (x ^ far) + (c ^ other)
                body(other, far, slot, columns(head))


def attended_kernel(pieces, factor, ids, q_ref, k_ref, v_ref, own_ref, got_ref, *outs):
    f, x, c = (ids[3], ids[1], ids[2])
    per = HEADS // pieces
    for r in range(pieces):
        for other, s_ref in ((0, own_ref), (1, got_ref)):
            for t in range(per // 2):
                inner = 2 * t + (c ^ other)
                head = lax.rem(f + r, pieces) * per + inner
                far = ((head >> 1) & 1) ^ x
                cols = columns(head)
                q, k, v = (q_ref[0, :, cols], k_ref[0, :, cols], v_ref[0, :, cols])
                scores = masked(dot(q, k, 1, 1))
                out = dot(q, s_ref[far, head >> 2], 1, 0) + dot(scores, v, 1, 0)
                outs[r][:, columns(inner)] = (factor * out).astype(BF16)


def query_grad_kernel(factor, ids, g_ref, k_ref, v_ref, own_ref, got_ref, out_ref):
    def body(other, far, slot, cols):
        g, k, v = (g_ref[0, :, cols], k_ref[0, :, cols], v_ref[0, :, cols])
        mixing = masked(dot(g, v, 1, 1))
        state = (own_ref, got_ref)[other][far, slot]
        out = dot(g, state, 1, 1) + dot(mixing, k, 1, 0)
        out_ref[0, :, cols] = (factor * out).astype(BF16)

    each_head(ids, body)


def key_value_grad_kernel(
    factor, ids, q_ref, k_ref, v_ref, g_ref, own_ref, got_ref, key_ref, value_ref
):
    def body(other, far, slot, cols):
        q, k = (q_ref[0, :, cols], k_ref[0, :, cols])
        v, g = (v_ref[0, :, cols], g_ref[0, :, cols])
        state = (own_ref, got_ref)[other][far, slot]
        mixing = masked(dot(g, v, 1, 1))
        scores = masked(dot(q, k, 1, 1))
        key = dot(v, state, 1, 1) + dot(mixing, q, 0, 0)
        value = dot(k, state, 1, 0) + dot(scores, g, 0, 0)
        key_ref[0, :, cols] = (factor * key).astype(BF16)
        value_ref[0, :, cols] = (factor * value).astype(BF16)

    each_head(ids, body)


def swap(value, distance, count):
    return lax.ppermute(value, "seq", [(i, i ^ distance) for i in range(count)])


def scan(mine, send, ids, count, reverse):
    x, c = (ids[1], ids[2])
    first_x = (1 - x if reverse else x).astype(F32)
    first_c = (1 - c if reverse else c).astype(F32)
    levels = count // PLANE
    pair = swap(send, 1, count).astype(F32)
    chip = mine + pair
    across = swap(chip[1].astype(BF16), 2, count).astype(F32)
    plane = (chip[0] + across).astype(BF16)
    before = jnp.zeros(plane.shape, F32)
    for step in range(1, levels):
        move = -PLANE * step if reverse else PLANE * step
        route = [(i, i + move) for i in range(count) if 0 <= i + move < count]
        before = before + lax.ppermute(plane, "seq", route).astype(F32)
    near = before + first_x * across
    far = swap((before + (1.0 - first_x) * chip[0]).astype(BF16), 2, count)
    chip_before = jnp.stack([near, far.astype(F32)])
    got = swap((chip_before + (1.0 - first_c) * mine).astype(BF16), 1, count)
    own = (chip_before + first_c * pair).astype(BF16)
    return own, got


def shift(value, r, count):
    return lax.ppermute(value, "fsdp", [(i, (i + r) % count) for i in range(count)])


def body(queries, key_vectors, value_vectors, out_grad, out_weight):
    seq_devices = lax.axis_size("seq")
    fsdp_devices = lax.axis_size("fsdp")
    batches, tokens, width = queries.shape
    rows = out_grad.shape[2] // seq_devices
    levels = seq_devices // PLANE
    piece = out_weight.shape[1]
    factor = 1.0 / math.sqrt(HEAD_DIM * tokens * seq_devices)
    grad_factor = 1.0 / math.sqrt(fsdp_devices * tokens * seq_devices)
    me = lax.axis_index("seq")
    ids = jnp.stack([me // PLANE, (me >> 1) & 1, me & 1, lax.axis_index("fsdp")]).astype(jnp.int32)
    half = (2, SLOTS, HEAD_DIM, HEAD_DIM)

    mine, send = call(state_kernel, ids, (key_vectors, value_vectors), [(half, F32), (half, BF16)])
    grads_all = [out_grad[0]] + [shift(out_grad[0], r, fsdp_devices) for r in range(1, fsdp_devices)]
    s_own, s_got = scan(mine, send, ids, seq_devices, False)

    attn_pieces = []
    for r in range(fsdp_devices):
        part = dot(grads_all[r], out_weight, 1, 0).astype(BF16)
        attn_pieces.append(part if r == 0 else shift(part, -r, fsdp_devices))

    def grad_states(ids, *refs):
        grad_state_kernel(fsdp_devices, ids, *refs)

    grad_attn, g_mine, g_send = call(
        grad_states,
        ids,
        (queries, *attn_pieces),
        [(queries.shape, BF16), (half, F32), (half, BF16)],
    )
    g_own, g_got = scan(g_mine, g_send, ids, seq_devices, True)

    def attended_heads(ids, *refs):
        attended_kernel(fsdp_devices, factor, ids, *refs)

    attended = call(
        attended_heads,
        ids,
        (queries, key_vectors, value_vectors, s_own, s_got),
        [((tokens, piece), BF16)] * fsdp_devices,
    )
    attended_all = [attended[0]] + [
        shift(attended[r], r, fsdp_devices) for r in range(1, fsdp_devices)
    ]

    def query_grads(ids, *refs):
        query_grad_kernel(factor, ids, *refs)

    (query_grad,) = call(
        query_grads,
        ids,
        (grad_attn, key_vectors, value_vectors, s_own, s_got),
        [(queries.shape, BF16)],
    )

    def key_value_grads(ids, *refs):
        key_value_grad_kernel(factor, ids, *refs)

    key_grad, value_grad = call(
        key_value_grads,
        ids,
        (queries, key_vectors, value_vectors, grad_attn, g_own, g_got),
        [(queries.shape, BF16)] * 2,
    )

    features = jnp.concatenate(grads_all).reshape(-1, levels, PLANE, rows)
    features = jnp.roll(features, -ids[0], axis=1)
    member = me % PLANE
    parts = [
        lax.dynamic_index_in_dim(features, member ^ j, 2, keepdims=False).reshape(-1, levels * rows)
        for j in range(PLANE)
    ]
    grads_plane = [parts[0]] + [swap(parts[j], j, seq_devices) for j in range(1, PLANE)]
    near = jnp.concatenate(attended_all)
    across = swap(near, 2, seq_devices)
    pair = swap(near, 1, seq_devices)
    diagonal = swap(across, 1, seq_devices)
    partial = dot(
        jnp.concatenate(grads_plane), jnp.concatenate([near, pair, across, diagonal]), 0, 0
    )
    weight_grad = partial[:rows]
    for r in range(1, levels):
        route = [(i, (i + PLANE * r) % seq_devices) for i in range(seq_devices)]
        chunk = partial[r * rows : (r + 1) * rows].astype(BF16)
        weight_grad = weight_grad + lax.ppermute(chunk, "seq", route).astype(F32)
    return (query_grad, key_grad, value_grad, weight_grad * grad_factor)


def solution(mesh):
    in_specs = (
        P("fsdp", "seq", None),
        P("fsdp", "seq", None),
        P("fsdp", "seq", None),
        P("fsdp", "seq", None),
        P(None, "fsdp"),
    )
    out_specs = (
        P("fsdp", "seq", None),
        P("fsdp", "seq", None),
        P("fsdp", "seq", None),
        P("seq", "fsdp"),
    )
    return jax.shard_map(body, mesh=mesh, in_specs=in_specs, out_specs=out_specs, check_vma=False)
```

```python
import math

import jax
import jax.numpy as jnp
from jax import lax
from jax.experimental import pallas as pl
from jax.experimental.pallas import tpu as pltpu
from jax.sharding import PartitionSpec as P

HEADS = 16
HEAD_DIM = 128
BLOCK = 128
PLANE = 4
SLOTS = HEADS // PLANE
F32 = jnp.float32
BF16 = jnp.bfloat16
RAN = ((8, 128), F32)
VMEM_LIMIT = 16 * 1024 * 1024


def dot(a, b, contract_a, contract_b):
    dims = (((contract_a,), (contract_b,)), ((), ()))
    return lax.dot_general(a, b, dims, preferred_element_type=F32)


def call(kernel, ids, arrays, outs, after=()):
    vmem = pl.BlockSpec(memory_space=pltpu.VMEM)
    first, last = (1 + len(arrays), 1 + len(arrays) + len(after))

    def run(*refs):
        kernel(*refs[:first], *refs[last:])

    return pl.pallas_call(
        run,
        out_shape=[jax.ShapeDtypeStruct(shape, dtype) for shape, dtype in outs],
        in_specs=[pl.BlockSpec(memory_space=pltpu.SMEM)]
        + [vmem] * len(arrays)
        + [pl.BlockSpec(memory_space=pl.ANY)] * len(after),
        out_specs=[vmem] * len(outs),
        compiler_params=pltpu.CompilerParams(vmem_limit_bytes=VMEM_LIMIT),
    )(ids, *arrays, *after)


def columns(head):
    return pl.ds(pl.multiple_of(head * HEAD_DIM, HEAD_DIM), HEAD_DIM)


def each_head(ids, body):
    x, c = (ids[1], ids[2])
    for other in range(2):
        for far in range(2):
            for slot in range(SLOTS):
                head = 4 * slot + 2 * (x ^ far) + (c ^ other)
                body(other, far, slot, columns(head))


def state_kernel(ids, a_ref, b_ref, mine_ref, send_ref):
    def body(other, far, slot, cols):
        state = dot(a_ref[0, :, cols], b_ref[0, :, cols], 0, 0)
        out = (mine_ref, send_ref)[other]
        out[far, slot] = state.astype(out.dtype)

    each_head(ids, body)


def grad_state_kernel(pieces, ids, a_ref, *refs):
    whole_ref, mine_ref, send_ref = refs[pieces:]
    width = refs[0].shape[1]
    for r in range(pieces):
        at = lax.rem(ids[3] + r, pieces) * width
        whole_ref[0, :, pl.ds(pl.multiple_of(at, HEAD_DIM), width)] = refs[r][...]
    state_kernel(ids, a_ref, whole_ref, mine_ref, send_ref)


def masked(scores):
    rows = lax.broadcasted_iota(jnp.int32, (BLOCK, BLOCK), 0)
    cols = lax.broadcasted_iota(jnp.int32, (BLOCK, BLOCK), 1)
    return jnp.where(rows >= cols, scores, 0.0).astype(BF16)


def attended_kernel(pieces, factor, ids, q_ref, k_ref, v_ref, own_ref, got_ref, *outs):
    f, x, c = (ids[3], ids[1], ids[2])
    per = HEADS // pieces
    for r in range(pieces):
        for other, s_ref in ((0, own_ref), (1, got_ref)):
            for t in range(per // 2):
                inner = 2 * t + (c ^ other)
                head = lax.rem(f + r, pieces) * per + inner
                far = ((head >> 1) & 1) ^ x
                cols = columns(head)
                q, k, v = (q_ref[0, :, cols], k_ref[0, :, cols], v_ref[0, :, cols])
                scores = masked(dot(q, k, 1, 1))
                out = dot(q, s_ref[far, head >> 2], 1, 0) + dot(scores, v, 1, 0)
                outs[r][:, columns(inner)] = (factor * out).astype(BF16)


def block_kernel(
    factor,
    ids,
    q_ref,
    k_ref,
    v_ref,
    g_ref,
    own_ref,
    got_ref,
    query_ref,
    key_ref,
    value_ref,
    ran_ref,
):
    def body(other, far, slot, cols):
        q, k = (q_ref[0, :, cols], k_ref[0, :, cols])
        v, g = (v_ref[0, :, cols], g_ref[0, :, cols])
        mixing = masked(dot(g, v, 1, 1))
        scores = masked(dot(q, k, 1, 1))
        state = (own_ref, got_ref)[other][far, slot]
        query = dot(g, state, 1, 1) + dot(mixing, k, 1, 0)
        query_ref[0, :, cols] = (factor * query).astype(BF16)
        key_ref[:, cols] = dot(mixing, q, 0, 0)
        value_ref[:, cols] = dot(scores, g, 0, 0)

    each_head(ids, body)
    ran_ref[...] = jnp.zeros_like(ran_ref)


def later_kernel(
    factor, ids, k_ref, v_ref, key_in, value_in, own_ref, got_ref, key_ref, value_ref
):
    def body(other, far, slot, cols):
        k, v = (k_ref[0, :, cols], v_ref[0, :, cols])
        state = (own_ref, got_ref)[other][far, slot]
        key = dot(v, state, 1, 1) + key_in[:, cols]
        value = dot(k, state, 1, 0) + value_in[:, cols]
        key_ref[0, :, cols] = (factor * key).astype(BF16)
        value_ref[0, :, cols] = (factor * value).astype(BF16)

    each_head(ids, body)


def features_kernel(levels, ids, in_ref, here_ref, there_ref):
    z, member = (ids[0], 2 * ids[1] + ids[2])
    rows = in_ref.shape[1] // (levels * PLANE)
    for j in range(PLANE):
        out = (here_ref, there_ref)[j // 2]
        for step in range(levels):
            at = ((z ^ step) * PLANE + (member ^ j)) * rows
            block = in_ref[:, pl.ds(pl.multiple_of(at, HEAD_DIM), rows)]
            out[j % 2, :, step * rows : (step + 1) * rows] = block


def features(grads, ids, levels, after=()):
    tokens, width = grads.shape
    rows = width // (levels * PLANE)
    if rows % HEAD_DIM == 0:

        def run(ids, *refs):
            features_kernel(levels, ids, *refs)

        return call(run, ids, (grads,), [((2, tokens, levels * rows), BF16)] * 2, after)
    order = jnp.arange(levels) ^ ids[0]
    members = jnp.arange(PLANE) ^ (2 * ids[1] + ids[2])
    parts = jnp.take(grads.reshape(tokens, levels, PLANE, rows), order, axis=1)
    parts = jnp.take(parts, members, axis=2).transpose(2, 0, 1, 3)
    parts = parts.reshape(PLANE, tokens, levels * rows)
    return parts[:2], parts[2:]


def chip_rows_kernel(ids, here_ref, there_ref, *outs):
    tokens = here_ref.shape[1]
    for core, out in enumerate(outs):
        out[:tokens] = here_ref[core]
        out[tokens:] = there_ref[core]


def stack_kernel(ids, *refs):
    rows = refs[0].shape[0]
    for at, ref in enumerate(refs[:-1]):
        refs[-1][at * rows : (at + 1) * rows] = ref[...]


def swap(value, distance, count):
    return lax.ppermute(value, "seq", [(i, i ^ distance) for i in range(count)])


def shift(value, r, count):
    return lax.ppermute(value, "fsdp", [(i, (i + r) % count) for i in range(count)])


def shift_across(value, r, count, devices):
    route = [
        (i * count + f, (i ^ 2) * count + (f + r) % count) for i in range(devices) for f in range(count)
    ]
    return lax.ppermute(value, ("seq", "fsdp"), route)


def chip_kernel(ids, mine_ref, pair_ref, near_ref, send_ref):
    near_ref[...] = mine_ref[0] + pair_ref[0].astype(F32)
    send_ref[...] = (mine_ref[1] + pair_ref[1].astype(F32)).astype(BF16)


def sum_kernel(ids, a_ref, b_ref, out_ref):
    out_ref[...] = (a_ref[...].astype(F32) + b_ref[...].astype(F32)).astype(BF16)


def before_kernel(reverse, ids, chip_ref, across_ref, *refs):
    near_ref, send_ref = refs[-2:]
    before = refs[0][...].astype(F32)
    for ref in refs[1:-2]:
        before = before + ref[...].astype(F32)
    second = (1 - ids[1] if reverse else ids[1]) == 1
    near_ref[...] = before + jnp.where(second, across_ref[...].astype(F32), 0.0)
    send_ref[...] = (before + jnp.where(second, 0.0, chip_ref[...])).astype(BF16)


def core_kernel(reverse, ids, near_ref, far_ref, mine_ref, pair_ref, own_ref, send_ref):
    second = (1 - ids[2] if reverse else ids[2]) == 1
    for at, ref in ((0, near_ref), (1, far_ref)):
        before = ref[...].astype(F32)
        own = before + jnp.where(second, pair_ref[at].astype(F32), 0.0)
        send = before + jnp.where(second, 0.0, mine_ref[at])
        own_ref[at] = own.astype(BF16)
        send_ref[at] = send.astype(BF16)


class Scan:
    def __init__(self, mine, send, ids, count, reverse, doubling):
        self.mine, self.ids, self.count = (mine, ids, count)
        self.reverse, self.doubling = (reverse, doubling)
        self.quarter = (SLOTS, HEAD_DIM, HEAD_DIM)
        self.pair = swap(send, 1, count)

    def chip(self, after=()):
        outs = [(self.quarter, F32), (self.quarter, BF16)]
        self.total, to_x = call(chip_kernel, self.ids, (self.mine, self.pair), outs, after)
        self.across = swap(to_x, 2, self.count)
        return self.total

    def along(self, value, step):
        move = -PLANE * step if self.reverse else PLANE * step
        route = [(i, i + move) for i in range(self.count) if 0 <= i + move < self.count]
        return lax.ppermute(value, "seq", route)

    def plane(self, after=()):
        outs = [(self.quarter, BF16)]
        (self.summed,) = call(sum_kernel, self.ids, (self.total, self.across), outs, after)
        steps = [1] if self.doubling else range(1, self.count // PLANE)
        self.got = [self.along(self.summed, step) for step in steps]
        return self.summed

    def double(self, after=()):
        step = 2
        while step < self.count // PLANE:
            outs = [(self.quarter, BF16)]
            (self.summed,) = call(sum_kernel, self.ids, (self.summed, self.got[-1]), outs, after)
            self.got.append(self.along(self.summed, step))
            step *= 2
        return self.summed

    def before(self, after=()):
        def befores(ids, *refs):
            before_kernel(self.reverse, ids, *refs)

        outs = [(self.quarter, F32), (self.quarter, BF16)]
        arrays = (self.total, self.across, *self.got)
        self.near, to_x = call(befores, self.ids, arrays, outs, after)
        self.far = swap(to_x, 2, self.count)
        return self.near

    def core(self, after=()):
        def cores(ids, *refs):
            core_kernel(self.reverse, ids, *refs)

        outs = [((2, *self.quarter), BF16)] * 2
        arrays = (self.near, self.far, self.mine, self.pair)
        own, to_core = call(cores, self.ids, arrays, outs, after)
        return own, swap(to_core, 1, self.count)


def body(queries, key_vectors, value_vectors, out_grad, out_weight):
    seq_devices = lax.axis_size("seq")
    fsdp_devices = lax.axis_size("fsdp")
    batches, tokens, width = queries.shape
    rows = out_grad.shape[2] // seq_devices
    levels = seq_devices // PLANE
    piece = out_weight.shape[1]
    factor = 1.0 / math.sqrt(HEAD_DIM * tokens * seq_devices)
    grad_factor = 1.0 / math.sqrt(fsdp_devices * tokens * seq_devices)
    me = lax.axis_index("seq")
    ids = jnp.stack([me // PLANE, (me >> 1) & 1, me & 1, lax.axis_index("fsdp")]).astype(jnp.int32)
    half = (2, SLOTS, HEAD_DIM, HEAD_DIM)
    others = range(1, fsdp_devices)

    grads_own = out_grad[0]
    grads_got = [shift(grads_own, r, fsdp_devices) for r in others]
    mine, send = call(state_kernel, ids, (key_vectors, value_vectors), [(half, F32), (half, BF16)])
    s_scan = Scan(mine, send, ids, seq_devices, False, False)
    s_total = s_scan.chip()
    attn_own = dot(grads_own, out_weight, 1, 0).astype(BF16)
    here, there = features(grads_own, ids, levels, after=(s_total,))
    there = swap(there, 2, seq_devices)
    s_plane = s_scan.plane(after=(attn_own,))
    attn_got = [dot(grads, out_weight, 1, 0).astype(BF16) for grads in grads_got]
    attn_back = [shift(attn_got[r - 1], -r, fsdp_devices) for r in others]
    mine_rows, send_rows = call(
        chip_rows_kernel,
        ids,
        (here, there),
        [((2 * tokens, levels * rows), BF16)] * 2,
    )
    s_near = s_scan.before(after=(*attn_got, mine_rows))
    rows_own = jnp.stack([mine_rows, swap(send_rows, 1, seq_devices)])
    rows_all = [rows_own] + [shift(rows_own, r, fsdp_devices) for r in others]
    s_own, s_got = s_scan.core(after=attn_back)

    def grad_states(ids, *refs):
        grad_state_kernel(fsdp_devices, ids, *refs)

    grad_attn, g_mine, g_send = call(
        grad_states,
        ids,
        (queries, attn_own, *attn_back),
        [(queries.shape, BF16), (half, F32), (half, BF16)],
        after=(s_own,),
    )

    g_scan = Scan(g_mine, g_send, ids, seq_devices, True, True)
    g_scan.chip()

    def attended_heads(ids, *refs):
        attended_kernel(fsdp_devices, factor, ids, *refs)

    attended = call(
        attended_heads,
        ids,
        (queries, key_vectors, value_vectors, s_own, s_got),
        [((tokens, piece), BF16)] * fsdp_devices,
        after=(g_mine,),
    )
    near = [attended[0]] + [shift(attended[r], r, fsdp_devices) for r in others]
    across = [swap(attended[0], 2, seq_devices)]
    across += [shift_across(attended[r], r, fsdp_devices, seq_devices) for r in others]

    g_plane = g_scan.plane(after=(attended[0], *rows_all[1:]))

    def blocks(ids, *refs):
        block_kernel(factor, ids, *refs)

    flat = (tokens, width)
    query_grad, key_part, value_part, blocks_ran = call(
        blocks,
        ids,
        (queries, key_vectors, value_vectors, grad_attn, s_own, s_got),
        [(queries.shape, BF16), (flat, F32), (flat, F32), RAN],
        after=(g_plane,),
    )
    g_double = g_scan.double()
    g_near = g_scan.before()

    (near,) = call(
        stack_kernel,
        ids,
        [part for pair in zip(near, across) for part in pair],
        [((2 * fsdp_devices * tokens, piece), BF16)],
        after=(blocks_ran, g_double, *rows_all[1:]),
    )
    grads_rows = jnp.concatenate([part[core] for core in range(2) for part in rows_all])
    attended_all = jnp.concatenate([near, swap(near, 1, seq_devices)])
    partial = dot(grads_rows, attended_all, 0, 0)
    chunks = [partial[k * rows : (k + 1) * rows].astype(BF16) for k in range(levels)]
    got = [swap(chunks[k], PLANE * k, seq_devices) for k in range(1, levels)]
    g_own, g_got = g_scan.core(after=got[:1])

    def later(ids, *refs):
        later_kernel(factor, ids, *refs)

    key_grad, value_grad = call(
        later,
        ids,
        (key_vectors, value_vectors, key_part, value_part, g_own, g_got),
        [(queries.shape, BF16)] * 2,
    )
    weight_grad = partial[:rows]
    for chunk in got:
        weight_grad = weight_grad + chunk.astype(F32)
    return (query_grad, key_grad, value_grad, weight_grad * grad_factor)


def solution(mesh):
    in_specs = (
        P("fsdp", "seq", None),
        P("fsdp", "seq", None),
        P("fsdp", "seq", None),
        P("fsdp", "seq", None),
        P(None, "fsdp"),
    )
    out_specs = (
        P("fsdp", "seq", None),
        P("fsdp", "seq", None),
        P("fsdp", "seq", None),
        P("seq", "fsdp"),
    )
    return jax.shard_map(body, mesh=mesh, in_specs=in_specs, out_specs=out_specs, check_vma=False)
```

```python
import math

import jax
import jax.numpy as jnp
from jax import lax
from jax.experimental import pallas as pl
from jax.experimental.pallas import tpu as pltpu
from jax.sharding import PartitionSpec as P

HEADS = 16
HEAD_DIM = 128
BLOCK = 128
PLANE = 4
SLOTS = HEADS // PLANE
F32 = jnp.float32
BF16 = jnp.bfloat16
RAN = ((8, 128), F32)
VMEM_LIMIT = 16 * 1024 * 1024


def dot(a, b, contract_a, contract_b):
    dims = (((contract_a,), (contract_b,)), ((), ()))
    return lax.dot_general(a, b, dims, preferred_element_type=F32)


def call(kernel, ids, arrays, outs, after=()):
    vmem = pl.BlockSpec(memory_space=pltpu.VMEM)
    first, last = (1 + len(arrays), 1 + len(arrays) + len(after))

    def run(*refs):
        kernel(*refs[:first], *refs[last:])

    return pl.pallas_call(
        run,
        out_shape=[jax.ShapeDtypeStruct(shape, dtype) for shape, dtype in outs],
        in_specs=[pl.BlockSpec(memory_space=pltpu.SMEM)]
        + [vmem] * len(arrays)
        + [pl.BlockSpec(memory_space=pl.ANY)] * len(after),
        out_specs=[vmem] * len(outs),
        compiler_params=pltpu.CompilerParams(vmem_limit_bytes=VMEM_LIMIT),
    )(ids, *arrays, *after)


def columns(head):
    return pl.ds(pl.multiple_of(head * HEAD_DIM, HEAD_DIM), HEAD_DIM)


def each_head(ids, body):
    x, c = (ids[1], ids[2])
    for other in range(2):
        for far in range(2):
            for slot in range(SLOTS):
                head = 4 * slot + 2 * (x ^ far) + (c ^ other)
                body(other, far, slot, columns(head))


def state_kernel(ids, a_ref, b_ref, mine_ref, send_ref):
    def body(other, far, slot, cols):
        state = dot(a_ref[0, :, cols], b_ref[0, :, cols], 0, 0)
        out = (mine_ref, send_ref)[other]
        out[far, slot] = state.astype(out.dtype)

    each_head(ids, body)


def grad_state_kernel(pieces, ids, a_ref, *refs):
    whole_ref, mine_ref, send_ref = refs[pieces:]
    width = refs[0].shape[1]
    for r in range(pieces):
        at = lax.rem(ids[3] + r, pieces) * width
        whole_ref[0, :, pl.ds(pl.multiple_of(at, HEAD_DIM), width)] = refs[r][...]
    state_kernel(ids, a_ref, whole_ref, mine_ref, send_ref)


def masked(scores):
    rows = lax.broadcasted_iota(jnp.int32, (BLOCK, BLOCK), 0)
    cols = lax.broadcasted_iota(jnp.int32, (BLOCK, BLOCK), 1)
    return jnp.where(rows >= cols, scores, 0.0).astype(BF16)


def attended_kernel(pieces, factor, ids, q_ref, k_ref, v_ref, own_ref, got_ref, *outs):
    f, x, c = (ids[3], ids[1], ids[2])
    per = HEADS // pieces
    for r in range(pieces):
        for other, s_ref in ((0, own_ref), (1, got_ref)):
            for t in range(per // 2):
                inner = 2 * t + (c ^ other)
                head = lax.rem(f + r, pieces) * per + inner
                far = ((head >> 1) & 1) ^ x
                cols = columns(head)
                q, k, v = (q_ref[0, :, cols], k_ref[0, :, cols], v_ref[0, :, cols])
                scores = masked(dot(q, k, 1, 1))
                out = dot(q, s_ref[far, head >> 2], 1, 0) + dot(scores, v, 1, 0)
                outs[r][:, columns(inner)] = (factor * out).astype(BF16)


def block_kernel(
    factor,
    ids,
    q_ref,
    k_ref,
    v_ref,
    g_ref,
    own_ref,
    got_ref,
    query_ref,
    key_ref,
    value_ref,
    ran_ref,
):
    def body(other, far, slot, cols):
        q, k = (q_ref[0, :, cols], k_ref[0, :, cols])
        v, g = (v_ref[0, :, cols], g_ref[0, :, cols])
        mixing = masked(dot(g, v, 1, 1))
        scores = masked(dot(q, k, 1, 1))
        state = (own_ref, got_ref)[other][far, slot]
        query = dot(g, state, 1, 1) + dot(mixing, k, 1, 0)
        query_ref[0, :, cols] = (factor * query).astype(BF16)
        key_ref[:, cols] = dot(mixing, q, 0, 0)
        value_ref[:, cols] = dot(scores, g, 0, 0)

    each_head(ids, body)
    ran_ref[...] = jnp.zeros_like(ran_ref)


def later_kernel(
    factor, ids, k_ref, v_ref, key_in, value_in, own_ref, got_ref, key_ref, value_ref
):
    def body(other, far, slot, cols):
        k, v = (k_ref[0, :, cols], v_ref[0, :, cols])
        state = (own_ref, got_ref)[other][far, slot]
        key = dot(v, state, 1, 1) + key_in[:, cols]
        value = dot(k, state, 1, 0) + value_in[:, cols]
        key_ref[0, :, cols] = (factor * key).astype(BF16)
        value_ref[0, :, cols] = (factor * value).astype(BF16)

    each_head(ids, body)


def features_kernel(levels, ids, in_ref, here_ref, there_ref):
    z, member = (ids[0], 2 * ids[1] + ids[2])
    rows = in_ref.shape[1] // (levels * PLANE)
    for j in range(PLANE):
        out = (here_ref, there_ref)[j // 2]
        for step in range(levels):
            at = ((z ^ step) * PLANE + (member ^ j)) * rows
            block = in_ref[:, pl.ds(pl.multiple_of(at, HEAD_DIM), rows)]
            out[j % 2, :, step * rows : (step + 1) * rows] = block


def features(grads, ids, levels, after=()):
    tokens, width = grads.shape
    rows = width // (levels * PLANE)
    if rows % HEAD_DIM == 0:

        def run(ids, *refs):
            features_kernel(levels, ids, *refs)

        return call(run, ids, (grads,), [((2, tokens, levels * rows), BF16)] * 2, after)
    order = jnp.arange(levels) ^ ids[0]
    members = jnp.arange(PLANE) ^ (2 * ids[1] + ids[2])
    parts = jnp.take(grads.reshape(tokens, levels, PLANE, rows), order, axis=1)
    parts = jnp.take(parts, members, axis=2).transpose(2, 0, 1, 3)
    parts = parts.reshape(PLANE, tokens, levels * rows)
    return parts[:2], parts[2:]


def chip_rows_kernel(ids, here_ref, there_ref, *outs):
    tokens = here_ref.shape[1]
    for core, out in enumerate(outs):
        out[:tokens] = here_ref[core]
        out[tokens:] = there_ref[core]


def chip_rows(here, there, ids):
    shape = (2 * here.shape[1], here.shape[2])
    return call(chip_rows_kernel, ids, (here, there), [(shape, BF16)] * 2)


def stack_kernel(ids, *refs):
    rows = refs[0].shape[0]
    for at, ref in enumerate(refs[:-1]):
        refs[-1][at * rows : (at + 1) * rows] = ref[...]


def swap(value, distance, count):
    return lax.ppermute(value, "seq", [(i, i ^ distance) for i in range(count)])


def shift(value, r, count):
    return lax.ppermute(value, "fsdp", [(i, (i + r) % count) for i in range(count)])


def shift_across(value, r, count, devices):
    route = [
        (i * count + f, (i ^ 2) * count + (f + r) % count) for i in range(devices) for f in range(count)
    ]
    return lax.ppermute(value, ("seq", "fsdp"), route)


def chip_kernel(ids, mine_ref, pair_ref, near_ref, send_ref):
    near_ref[...] = mine_ref[0] + pair_ref[0].astype(F32)
    send_ref[...] = (mine_ref[1] + pair_ref[1].astype(F32)).astype(BF16)


def sum_kernel(ids, a_ref, b_ref, out_ref):
    out_ref[...] = (a_ref[...].astype(F32) + b_ref[...].astype(F32)).astype(BF16)


def before_kernel(reverse, ids, chip_ref, across_ref, *refs):
    near_ref, send_ref = refs[-2:]
    before = refs[0][...].astype(F32)
    for ref in refs[1:-2]:
        before = before + ref[...].astype(F32)
    second = (1 - ids[1] if reverse else ids[1]) == 1
    near_ref[...] = before + jnp.where(second, across_ref[...].astype(F32), 0.0)
    send_ref[...] = (before + jnp.where(second, 0.0, chip_ref[...])).astype(BF16)


def core_kernel(reverse, ids, near_ref, far_ref, mine_ref, pair_ref, own_ref, send_ref):
    second = (1 - ids[2] if reverse else ids[2]) == 1
    for at, ref in ((0, near_ref), (1, far_ref)):
        before = ref[...].astype(F32)
        own = before + jnp.where(second, pair_ref[at].astype(F32), 0.0)
        send = before + jnp.where(second, 0.0, mine_ref[at])
        own_ref[at] = own.astype(BF16)
        send_ref[at] = send.astype(BF16)


class Scan:
    def __init__(self, mine, send, ids, count, reverse, doubling):
        self.mine, self.ids, self.count = (mine, ids, count)
        self.reverse, self.doubling = (reverse, doubling)
        self.quarter = (SLOTS, HEAD_DIM, HEAD_DIM)
        self.pair = swap(send, 1, count)

    def chip(self, after=()):
        outs = [(self.quarter, F32), (self.quarter, BF16)]
        self.total, to_x = call(chip_kernel, self.ids, (self.mine, self.pair), outs, after)
        self.across = swap(to_x, 2, self.count)
        return self.total

    def along(self, value, step):
        move = -PLANE * step if self.reverse else PLANE * step
        route = [(i, i + move) for i in range(self.count) if 0 <= i + move < self.count]
        return lax.ppermute(value, "seq", route)

    def plane(self, after=()):
        outs = [(self.quarter, BF16)]
        (self.summed,) = call(sum_kernel, self.ids, (self.total, self.across), outs, after)
        steps = [1] if self.doubling else range(self.count // PLANE - 1, 0, -1)
        self.got = [self.along(self.summed, step) for step in steps]
        return self.summed

    def double(self, after=()):
        step = 2
        while step < self.count // PLANE:
            outs = [(self.quarter, BF16)]
            (self.summed,) = call(sum_kernel, self.ids, (self.summed, self.got[-1]), outs, after)
            self.got.append(self.along(self.summed, step))
            step *= 2
        return self.summed

    def before(self, after=()):
        def befores(ids, *refs):
            before_kernel(self.reverse, ids, *refs)

        outs = [(self.quarter, F32), (self.quarter, BF16)]
        arrays = (self.total, self.across, *self.got)
        self.near, to_x = call(befores, self.ids, arrays, outs, after)
        self.far = swap(to_x, 2, self.count)
        return self.near

    def core(self, after=()):
        def cores(ids, *refs):
            core_kernel(self.reverse, ids, *refs)

        outs = [((2, *self.quarter), BF16)] * 2
        arrays = (self.near, self.far, self.mine, self.pair)
        own, to_core = call(cores, self.ids, arrays, outs, after)
        return own, swap(to_core, 1, self.count)


def body(queries, key_vectors, value_vectors, out_grad, out_weight):
    seq_devices = lax.axis_size("seq")
    fsdp_devices = lax.axis_size("fsdp")
    batches, tokens, width = queries.shape
    rows = out_grad.shape[2] // seq_devices
    levels = seq_devices // PLANE
    piece = out_weight.shape[1]
    factor = 1.0 / math.sqrt(HEAD_DIM * tokens * seq_devices)
    grad_factor = 1.0 / math.sqrt(fsdp_devices * tokens * seq_devices)
    me = lax.axis_index("seq")
    ids = jnp.stack([me // PLANE, (me >> 1) & 1, me & 1, lax.axis_index("fsdp")]).astype(jnp.int32)
    half = (2, SLOTS, HEAD_DIM, HEAD_DIM)
    others = range(1, fsdp_devices)

    grads_own = out_grad[0]
    grads_got = [shift(grads_own, r, fsdp_devices) for r in others]
    mine, send = call(state_kernel, ids, (key_vectors, value_vectors), [(half, F32), (half, BF16)])
    s_scan = Scan(mine, send, ids, seq_devices, False, False)
    s_total = s_scan.chip()
    attn_own = dot(grads_own, out_weight, 1, 0).astype(BF16)
    here, there = features(grads_own, ids, levels, after=(s_total,))
    there = swap(there, 2, seq_devices)
    s_plane = s_scan.plane(after=(attn_own,))
    attn_got = [dot(grads, out_weight, 1, 0).astype(BF16) for grads in grads_got]
    attn_back = [shift(attn_got[r - 1], -r, fsdp_devices) for r in others]
    rows_own = chip_rows(here, there, ids)
    s_near = s_scan.before(after=(*attn_got, rows_own[0]))
    here_got, there_got = features(jnp.concatenate(grads_got), ids, levels, after=(s_near,))
    there_got = swap(there_got, 2, seq_devices)
    s_own, s_got = s_scan.core()

    def grad_states(ids, *refs):
        grad_state_kernel(fsdp_devices, ids, *refs)

    grad_attn, g_mine, g_send = call(
        grad_states,
        ids,
        (queries, attn_own, *attn_back),
        [(queries.shape, BF16), (half, F32), (half, BF16)],
        after=(s_own,),
    )

    g_scan = Scan(g_mine, g_send, ids, seq_devices, True, True)
    g_scan.chip(after=(there_got,))

    def attended_heads(ids, *refs):
        attended_kernel(fsdp_devices, factor, ids, *refs)

    attended = call(
        attended_heads,
        ids,
        (queries, key_vectors, value_vectors, s_own, s_got),
        [((tokens, piece), BF16)] * fsdp_devices,
        after=(g_mine,),
    )
    near = [attended[0]] + [shift(attended[r], r, fsdp_devices) for r in others]
    across = [swap(attended[0], 2, seq_devices)]
    across += [shift_across(attended[r], r, fsdp_devices, seq_devices) for r in others]

    g_plane = g_scan.plane(after=attended[:1])

    def blocks(ids, *refs):
        block_kernel(factor, ids, *refs)

    flat = (tokens, width)
    query_grad, key_part, value_part, blocks_ran = call(
        blocks,
        ids,
        (queries, key_vectors, value_vectors, grad_attn, s_own, s_got),
        [(queries.shape, BF16), (flat, F32), (flat, F32), RAN],
        after=(g_plane,),
    )
    rows_got = chip_rows(here_got, there_got, ids)
    g_double = g_scan.double()
    g_near = g_scan.before()

    (near,) = call(
        stack_kernel,
        ids,
        (near[0], across[0], *near[1:], *across[1:]),
        [((2 * fsdp_devices * tokens, piece), BF16)],
        after=(blocks_ran, g_double, rows_got[0]),
    )
    grads_rows = jnp.concatenate(
        [rows_own[0], rows_got[0], swap(rows_own[1], 1, seq_devices), swap(rows_got[1], 1, seq_devices)]
    )
    attended_all = jnp.concatenate([near, swap(near, 1, seq_devices)])
    partial = dot(grads_rows, attended_all, 0, 0)
    chunks = [partial[k * rows : (k + 1) * rows].astype(BF16) for k in range(levels)]
    got = [swap(chunks[k], PLANE * k, seq_devices) for k in range(1, levels)]
    g_own, g_got = g_scan.core(after=got[:1])

    def later(ids, *refs):
        later_kernel(factor, ids, *refs)

    key_grad, value_grad = call(
        later,
        ids,
        (key_vectors, value_vectors, key_part, value_part, g_own, g_got),
        [(queries.shape, BF16)] * 2,
    )
    weight_grad = partial[:rows]
    for chunk in got:
        weight_grad = weight_grad + chunk.astype(F32)
    return (query_grad, key_grad, value_grad, weight_grad * grad_factor)


def solution(mesh):
    in_specs = (
        P("fsdp", "seq", None),
        P("fsdp", "seq", None),
        P("fsdp", "seq", None),
        P("fsdp", "seq", None),
        P(None, "fsdp"),
    )
    out_specs = (
        P("fsdp", "seq", None),
        P("fsdp", "seq", None),
        P("fsdp", "seq", None),
        P("seq", "fsdp"),
    )
    return jax.shard_map(body, mesh=mesh, in_specs=in_specs, out_specs=out_specs, check_vma=False)
```

```python
import math

import jax
import jax.numpy as jnp
from jax import lax
from jax.experimental import pallas as pl
from jax.experimental.pallas import tpu as pltpu
from jax.sharding import PartitionSpec as P

HEADS = 16
HEAD_DIM = 128
BLOCK = 128
PLANE = 4
SLOTS = HEADS // PLANE
F32 = jnp.float32
BF16 = jnp.bfloat16
RAN = ((8, 128), F32)
VMEM_LIMIT = 16 * 1024 * 1024


def dot(a, b, contract_a, contract_b):
    dims = (((contract_a,), (contract_b,)), ((), ()))
    return lax.dot_general(a, b, dims, preferred_element_type=F32)


def call(kernel, ids, arrays, outs, after=()):
    vmem = pl.BlockSpec(memory_space=pltpu.VMEM)
    first, last = (1 + len(arrays), 1 + len(arrays) + len(after))

    def run(*refs):
        kernel(*refs[:first], *refs[last:])

    return pl.pallas_call(
        run,
        out_shape=[jax.ShapeDtypeStruct(shape, dtype) for shape, dtype in outs],
        in_specs=[pl.BlockSpec(memory_space=pltpu.SMEM)]
        + [vmem] * len(arrays)
        + [pl.BlockSpec(memory_space=pl.ANY)] * len(after),
        out_specs=[vmem] * len(outs),
        compiler_params=pltpu.CompilerParams(vmem_limit_bytes=VMEM_LIMIT),
    )(ids, *arrays, *after)


def columns(head):
    return pl.ds(pl.multiple_of(head * HEAD_DIM, HEAD_DIM), HEAD_DIM)


def each_head(ids, body):
    x, c = (ids[1], ids[2])
    for other in range(2):
        for far in range(2):
            for slot in range(SLOTS):
                head = 4 * slot + 2 * (x ^ far) + (c ^ other)
                body(other, far, slot, columns(head))


def state_kernel(ids, a_ref, b_ref, mine_ref, send_ref):
    def body(other, far, slot, cols):
        state = dot(a_ref[0, :, cols], b_ref[0, :, cols], 0, 0)
        out = (mine_ref, send_ref)[other]
        out[far, slot] = state.astype(out.dtype)

    each_head(ids, body)


def grad_state_kernel(pieces, ids, a_ref, *refs):
    whole_ref, mine_ref, send_ref = refs[pieces:]
    width = refs[0].shape[1]
    for r in range(pieces):
        at = lax.rem(ids[3] + r, pieces) * width
        whole_ref[0, :, pl.ds(pl.multiple_of(at, HEAD_DIM), width)] = refs[r][...]
    state_kernel(ids, a_ref, whole_ref, mine_ref, send_ref)


def masked(scores):
    rows = lax.broadcasted_iota(jnp.int32, (BLOCK, BLOCK), 0)
    cols = lax.broadcasted_iota(jnp.int32, (BLOCK, BLOCK), 1)
    return jnp.where(rows >= cols, scores, 0.0).astype(BF16)


def attended_kernel(pieces, factor, ids, q_ref, k_ref, v_ref, own_ref, got_ref, *outs):
    f, x, c = (ids[3], ids[1], ids[2])
    per = HEADS // pieces
    for r in range(pieces):
        for other, s_ref in ((0, own_ref), (1, got_ref)):
            for t in range(per // 2):
                inner = 2 * t + (c ^ other)
                head = lax.rem(f + r, pieces) * per + inner
                far = ((head >> 1) & 1) ^ x
                cols = columns(head)
                q, k, v = (q_ref[0, :, cols], k_ref[0, :, cols], v_ref[0, :, cols])
                scores = masked(dot(q, k, 1, 1))
                out = dot(q, s_ref[far, head >> 2], 1, 0) + dot(scores, v, 1, 0)
                outs[r][:, columns(inner)] = (factor * out).astype(BF16)


def block_kernel(
    factor,
    ids,
    q_ref,
    k_ref,
    v_ref,
    g_ref,
    own_ref,
    got_ref,
    query_ref,
    key_ref,
    value_ref,
    ran_ref,
):
    def body(other, far, slot, cols):
        q, k = (q_ref[0, :, cols], k_ref[0, :, cols])
        v, g = (v_ref[0, :, cols], g_ref[0, :, cols])
        mixing = masked(dot(g, v, 1, 1))
        scores = masked(dot(q, k, 1, 1))
        state = (own_ref, got_ref)[other][far, slot]
        query = dot(g, state, 1, 1) + dot(mixing, k, 1, 0)
        query_ref[0, :, cols] = (factor * query).astype(BF16)
        key_ref[:, cols] = dot(mixing, q, 0, 0)
        value_ref[:, cols] = dot(scores, g, 0, 0)

    each_head(ids, body)
    ran_ref[...] = jnp.zeros_like(ran_ref)


def later_kernel(
    factor, ids, k_ref, v_ref, key_in, value_in, own_ref, got_ref, key_ref, value_ref
):
    def body(other, far, slot, cols):
        k, v = (k_ref[0, :, cols], v_ref[0, :, cols])
        state = (own_ref, got_ref)[other][far, slot]
        key = dot(v, state, 1, 1) + key_in[:, cols]
        value = dot(k, state, 1, 0) + value_in[:, cols]
        key_ref[0, :, cols] = (factor * key).astype(BF16)
        value_ref[0, :, cols] = (factor * value).astype(BF16)

    each_head(ids, body)


def features_kernel(levels, ids, in_ref, here_ref, there_ref):
    z, member = (ids[0], 2 * ids[1] + ids[2])
    rows = in_ref.shape[1] // (levels * PLANE)
    for j in range(PLANE):
        out = (here_ref, there_ref)[j // 2]
        for step in range(levels):
            at = ((z ^ step) * PLANE + (member ^ j)) * rows
            block = in_ref[:, pl.ds(pl.multiple_of(at, HEAD_DIM), rows)]
            out[j % 2, :, step * rows : (step + 1) * rows] = block


def features(grads, ids, levels, after=()):
    tokens, width = grads.shape
    rows = width // (levels * PLANE)
    if rows % HEAD_DIM == 0:

        def run(ids, *refs):
            features_kernel(levels, ids, *refs)

        return call(run, ids, (grads,), [((2, tokens, levels * rows), BF16)] * 2, after)
    order = jnp.arange(levels) ^ ids[0]
    members = jnp.arange(PLANE) ^ (2 * ids[1] + ids[2])
    parts = jnp.take(grads.reshape(tokens, levels, PLANE, rows), order, axis=1)
    parts = jnp.take(parts, members, axis=2).transpose(2, 0, 1, 3)
    parts = parts.reshape(PLANE, tokens, levels * rows)
    return parts[:2], parts[2:]


def chip_rows_kernel(ids, here_ref, there_ref, *outs):
    tokens = here_ref.shape[1]
    for core, out in enumerate(outs):
        out[:tokens] = here_ref[core]
        out[tokens:] = there_ref[core]


def chip_rows(here, there, ids):
    shape = (2 * here.shape[1], here.shape[2])
    return call(chip_rows_kernel, ids, (here, there), [(shape, BF16)] * 2)


def stack_kernel(ids, *refs):
    rows = refs[0].shape[0]
    for at, ref in enumerate(refs[:-1]):
        refs[-1][at * rows : (at + 1) * rows] = ref[...]


def swap(value, distance, count):
    return lax.ppermute(value, "seq", [(i, i ^ distance) for i in range(count)])


def shift(value, r, count):
    return lax.ppermute(value, "fsdp", [(i, (i + r) % count) for i in range(count)])


def shift_across(value, r, count, devices):
    route = [
        (i * count + f, (i ^ 2) * count + (f + r) % count) for i in range(devices) for f in range(count)
    ]
    return lax.ppermute(value, ("seq", "fsdp"), route)


def chip_kernel(ids, mine_ref, pair_ref, near_ref, send_ref):
    near_ref[...] = mine_ref[0] + pair_ref[0].astype(F32)
    send_ref[...] = (mine_ref[1] + pair_ref[1].astype(F32)).astype(BF16)


def sum_kernel(ids, a_ref, b_ref, out_ref):
    out_ref[...] = (a_ref[...].astype(F32) + b_ref[...].astype(F32)).astype(BF16)


def before_kernel(reverse, ids, chip_ref, across_ref, *refs):
    near_ref, send_ref = refs[-2:]
    before = refs[0][...].astype(F32)
    for ref in refs[1:-2]:
        before = before + ref[...].astype(F32)
    second = (1 - ids[1] if reverse else ids[1]) == 1
    near_ref[...] = before + jnp.where(second, across_ref[...].astype(F32), 0.0)
    send_ref[...] = (before + jnp.where(second, 0.0, chip_ref[...])).astype(BF16)


def core_kernel(reverse, ids, near_ref, far_ref, mine_ref, pair_ref, own_ref, send_ref):
    second = (1 - ids[2] if reverse else ids[2]) == 1
    for at, ref in ((0, near_ref), (1, far_ref)):
        before = ref[...].astype(F32)
        own = before + jnp.where(second, pair_ref[at].astype(F32), 0.0)
        send = before + jnp.where(second, 0.0, mine_ref[at])
        own_ref[at] = own.astype(BF16)
        send_ref[at] = send.astype(BF16)


class Scan:
    def __init__(self, mine, send, ids, count, reverse, doubling):
        self.mine, self.ids, self.count = (mine, ids, count)
        self.reverse, self.doubling = (reverse, doubling)
        self.quarter = (SLOTS, HEAD_DIM, HEAD_DIM)
        self.pair = swap(send, 1, count)

    def chip(self, after=()):
        outs = [(self.quarter, F32), (self.quarter, BF16)]
        self.total, to_x = call(chip_kernel, self.ids, (self.mine, self.pair), outs, after)
        self.across = swap(to_x, 2, self.count)
        return self.total

    def along(self, value, step):
        move = -PLANE * step if self.reverse else PLANE * step
        route = [(i, i + move) for i in range(self.count) if 0 <= i + move < self.count]
        return lax.ppermute(value, "seq", route)

    def plane(self, after=()):
        outs = [(self.quarter, BF16)]
        (self.summed,) = call(sum_kernel, self.ids, (self.total, self.across), outs, after)
        steps = [1] if self.doubling else range(self.count // PLANE - 1, 0, -1)
        self.got = [self.along(self.summed, step) for step in steps]
        return self.summed

    def double(self, after=()):
        step = 2
        while step < self.count // PLANE:
            outs = [(self.quarter, BF16)]
            (self.summed,) = call(sum_kernel, self.ids, (self.summed, self.got[-1]), outs, after)
            self.got.append(self.along(self.summed, step))
            step *= 2
        return self.summed

    def before(self, after=()):
        def befores(ids, *refs):
            before_kernel(self.reverse, ids, *refs)

        outs = [(self.quarter, F32), (self.quarter, BF16)]
        arrays = (self.total, self.across, *self.got)
        self.near, to_x = call(befores, self.ids, arrays, outs, after)
        self.far = swap(to_x, 2, self.count)
        return self.near

    def core(self, after=()):
        def cores(ids, *refs):
            core_kernel(self.reverse, ids, *refs)

        outs = [((2, *self.quarter), BF16)] * 2
        arrays = (self.near, self.far, self.mine, self.pair)
        own, to_core = call(cores, self.ids, arrays, outs, after)
        return own, swap(to_core, 1, self.count)


def body(queries, key_vectors, value_vectors, out_grad, out_weight):
    seq_devices = lax.axis_size("seq")
    fsdp_devices = lax.axis_size("fsdp")
    batches, tokens, width = queries.shape
    rows = out_grad.shape[2] // seq_devices
    levels = seq_devices // PLANE
    piece = out_weight.shape[1]
    factor = 1.0 / math.sqrt(HEAD_DIM * tokens * seq_devices)
    grad_factor = 1.0 / math.sqrt(fsdp_devices * tokens * seq_devices)
    me = lax.axis_index("seq")
    ids = jnp.stack([me // PLANE, (me >> 1) & 1, me & 1, lax.axis_index("fsdp")]).astype(jnp.int32)
    half = (2, SLOTS, HEAD_DIM, HEAD_DIM)
    others = range(1, fsdp_devices)

    grads_own = out_grad[0]
    grads_got = [shift(grads_own, r, fsdp_devices) for r in others]
    mine, send = call(state_kernel, ids, (key_vectors, value_vectors), [(half, F32), (half, BF16)])
    s_scan = Scan(mine, send, ids, seq_devices, False, False)
    s_total = s_scan.chip()
    attn_own = dot(grads_own, out_weight, 1, 0).astype(BF16)
    here, there = features(grads_own, ids, levels, after=(s_total,))
    there = swap(there, 2, seq_devices)
    s_plane = s_scan.plane(after=(attn_own,))
    attn_got = [dot(grads, out_weight, 1, 0).astype(BF16) for grads in grads_got]
    attn_back = [shift(attn_got[r - 1], -r, fsdp_devices) for r in others]
    rows_own = chip_rows(here, there, ids)
    rows_own_other = swap(rows_own[1], 1, seq_devices)
    s_near = s_scan.before(after=(*attn_got, rows_own[0]))
    here_got, there_got = features(jnp.concatenate(grads_got), ids, levels, after=(s_near,))
    there_got = swap(there_got, 2, seq_devices)
    s_own, s_got = s_scan.core()

    def grad_states(ids, *refs):
        grad_state_kernel(fsdp_devices, ids, *refs)

    grad_attn, g_mine, g_send = call(
        grad_states,
        ids,
        (queries, attn_own, *attn_back),
        [(queries.shape, BF16), (half, F32), (half, BF16)],
        after=(s_own,),
    )

    g_scan = Scan(g_mine, g_send, ids, seq_devices, True, True)
    g_total = g_scan.chip(after=(there_got,))

    def attended_heads(ids, *refs):
        attended_kernel(fsdp_devices, factor, ids, *refs)

    attended = call(
        attended_heads,
        ids,
        (queries, key_vectors, value_vectors, s_own, s_got),
        [((tokens, piece), BF16)] * fsdp_devices,
        after=(g_total, rows_own_other),
    )
    near = [attended[0]] + [shift(attended[r], r, fsdp_devices) for r in others]
    across = [swap(attended[0], 2, seq_devices)]
    across += [shift_across(attended[r], r, fsdp_devices, seq_devices) for r in others]

    g_plane = g_scan.plane(after=attended[:1])

    def blocks(ids, *refs):
        block_kernel(factor, ids, *refs)

    flat = (tokens, width)
    query_grad, key_part, value_part, blocks_ran = call(
        blocks,
        ids,
        (queries, key_vectors, value_vectors, grad_attn, s_own, s_got),
        [(queries.shape, BF16), (flat, F32), (flat, F32), RAN],
        after=(g_plane,),
    )
    rows_got = chip_rows(here_got, there_got, ids)
    g_double = g_scan.double(after=rows_got[:1])
    g_near = g_scan.before()

    (near,) = call(
        stack_kernel,
        ids,
        (near[0], across[0], *near[1:], *across[1:]),
        [((2 * fsdp_devices * tokens, piece), BF16)],
        after=(blocks_ran, g_double, rows_got[0]),
    )
    grads_rows = jnp.concatenate(
        [rows_own[0], rows_got[0], rows_own_other, swap(rows_got[1], 1, seq_devices)]
    )
    attended_all = jnp.concatenate([near, swap(near, 1, seq_devices)])
    partial = dot(grads_rows, attended_all, 0, 0)
    chunks = [partial[k * rows : (k + 1) * rows].astype(BF16) for k in range(levels)]
    got = [swap(chunks[k], PLANE * k, seq_devices) for k in range(1, levels)]
    g_own, g_got = g_scan.core(after=got[:2])

    def later(ids, *refs):
        later_kernel(factor, ids, *refs)

    key_grad, value_grad = call(
        later,
        ids,
        (key_vectors, value_vectors, key_part, value_part, g_own, g_got),
        [(queries.shape, BF16)] * 2,
    )
    weight_grad = partial[:rows]
    for chunk in got:
        weight_grad = weight_grad + chunk.astype(F32)
    return (query_grad, key_grad, value_grad, weight_grad * grad_factor)


def solution(mesh):
    in_specs = (
        P("fsdp", "seq", None),
        P("fsdp", "seq", None),
        P("fsdp", "seq", None),
        P("fsdp", "seq", None),
        P(None, "fsdp"),
    )
    out_specs = (
        P("fsdp", "seq", None),
        P("fsdp", "seq", None),
        P("fsdp", "seq", None),
        P("seq", "fsdp"),
    )
    return jax.shard_map(body, mesh=mesh, in_specs=in_specs, out_specs=out_specs, check_vma=False)
```

```python
import math

import jax
import jax.numpy as jnp
from jax import lax
from jax.experimental import pallas as pl
from jax.experimental.pallas import tpu as pltpu
from jax.sharding import PartitionSpec as P

HEADS = 16
HEAD_DIM = 128
BLOCK = 128
PLANE = 4
SLOTS = HEADS // PLANE
F32 = jnp.float32
BF16 = jnp.bfloat16
RAN = ((8, 128), F32)
VMEM_LIMIT = 16 * 1024 * 1024


def dot(a, b, contract_a, contract_b):
    dims = (((contract_a,), (contract_b,)), ((), ()))
    return lax.dot_general(a, b, dims, preferred_element_type=F32)


def call(kernel, ids, arrays, outs, after=(), stored=False, scratch=()):
    vmem = pl.BlockSpec(memory_space=pltpu.VMEM)
    first, last = (1 + len(arrays), 1 + len(arrays) + len(after))

    def run(*refs):
        kernel(*refs[:first], *refs[last:])

    return pl.pallas_call(
        run,
        out_shape=[jax.ShapeDtypeStruct(shape, dtype) for shape, dtype in outs],
        in_specs=[pl.BlockSpec(memory_space=pltpu.SMEM)]
        + [vmem] * len(arrays)
        + [pl.BlockSpec(memory_space=pl.ANY)] * len(after),
        out_specs=[pl.BlockSpec(memory_space=pl.ANY) if stored else vmem] * len(outs),
        scratch_shapes=scratch,
        compiler_params=pltpu.CompilerParams(vmem_limit_bytes=VMEM_LIMIT),
    )(ids, *arrays, *after)


def columns(head):
    return pl.ds(pl.multiple_of(head * HEAD_DIM, HEAD_DIM), HEAD_DIM)


def each_head(ids, body):
    x, c = (ids[1], ids[2])
    for other in range(2):
        for far in range(2):
            for slot in range(SLOTS):
                head = 4 * slot + 2 * (x ^ far) + (c ^ other)
                body(other, far, slot, columns(head))


def state_kernel(ids, a_ref, b_ref, mine_ref, send_ref):
    def body(other, far, slot, cols):
        state = dot(a_ref[0, :, cols], b_ref[0, :, cols], 0, 0)
        out = (mine_ref, send_ref)[other]
        out[far, slot] = state.astype(out.dtype)

    each_head(ids, body)


def grad_state_kernel(pieces, ids, a_ref, *refs):
    whole_ref, mine_ref, send_ref = refs[pieces:]
    width = refs[0].shape[1]
    for r in range(pieces):
        at = lax.rem(ids[3] + r, pieces) * width
        whole_ref[0, :, pl.ds(pl.multiple_of(at, HEAD_DIM), width)] = refs[r][...]
    state_kernel(ids, a_ref, whole_ref, mine_ref, send_ref)


def masked(scores):
    rows = lax.broadcasted_iota(jnp.int32, (BLOCK, BLOCK), 0)
    cols = lax.broadcasted_iota(jnp.int32, (BLOCK, BLOCK), 1)
    return jnp.where(rows >= cols, scores, 0.0).astype(BF16)


def attended_kernel(pieces, factor, ids, q_ref, k_ref, v_ref, own_ref, got_ref, *outs):
    f, x, c = (ids[3], ids[1], ids[2])
    per = HEADS // pieces
    for r in range(pieces):
        for other, s_ref in ((0, own_ref), (1, got_ref)):
            for t in range(per // 2):
                inner = 2 * t + (c ^ other)
                head = lax.rem(f + r, pieces) * per + inner
                far = ((head >> 1) & 1) ^ x
                cols = columns(head)
                q, k, v = (q_ref[0, :, cols], k_ref[0, :, cols], v_ref[0, :, cols])
                scores = masked(dot(q, k, 1, 1))
                out = dot(q, s_ref[far, head >> 2], 1, 0) + dot(scores, v, 1, 0)
                outs[r][:, columns(inner)] = (factor * out).astype(BF16)


def block_kernel(
    factor,
    ids,
    q_ref,
    k_ref,
    v_ref,
    g_ref,
    own_ref,
    got_ref,
    query_ref,
    key_ref,
    value_ref,
    ran_ref,
):
    def body(other, far, slot, cols):
        q, k = (q_ref[0, :, cols], k_ref[0, :, cols])
        v, g = (v_ref[0, :, cols], g_ref[0, :, cols])
        mixing = masked(dot(g, v, 1, 1))
        scores = masked(dot(q, k, 1, 1))
        state = (own_ref, got_ref)[other][far, slot]
        query = dot(g, state, 1, 1) + dot(mixing, k, 1, 0)
        query_ref[0, :, cols] = (factor * query).astype(BF16)
        key_ref[:, cols] = dot(mixing, q, 0, 0)
        value_ref[:, cols] = dot(scores, g, 0, 0)

    each_head(ids, body)
    ran_ref[...] = jnp.zeros_like(ran_ref)


def later_kernel(
    factor, ids, k_ref, v_ref, key_in, value_in, own_ref, got_ref, key_out, value_out, key_ref, value_ref, sems
):
    x, c = (ids[1], ids[2])
    width = PLANE * HEAD_DIM
    copies = []
    for slot in range(SLOTS):
        for other in range(2):
            for far in range(2):
                cols = columns(4 * slot + 2 * (x ^ far) + (c ^ other))
                k, v = (k_ref[0, :, cols], v_ref[0, :, cols])
                state = (own_ref, got_ref)[other][far, slot]
                key = dot(v, state, 1, 1) + key_in[:, cols]
                value = dot(k, state, 1, 0) + value_in[:, cols]
                key_ref[0, :, cols] = (factor * key).astype(BF16)
                value_ref[0, :, cols] = (factor * value).astype(BF16)
        done = pl.ds(slot * width, width)
        for at, (ref, out) in enumerate(((key_ref, key_out), (value_ref, value_out))):
            copy = pltpu.make_async_copy(ref.at[:, :, done], out.at[:, :, done], sems.at[at, slot])
            copy.start()
            copies.append(copy)
    for copy in copies:
        copy.wait()


def features_kernel(levels, ids, in_ref, here_ref, there_ref):
    z, member = (ids[0], 2 * ids[1] + ids[2])
    rows = in_ref.shape[1] // (levels * PLANE)
    for j in range(PLANE):
        out = (here_ref, there_ref)[j // 2]
        for step in range(levels):
            at = ((z ^ step) * PLANE + (member ^ j)) * rows
            block = in_ref[:, pl.ds(pl.multiple_of(at, HEAD_DIM), rows)]
            out[j % 2, :, step * rows : (step + 1) * rows] = block


def features(grads, ids, levels, after=()):
    tokens, width = grads.shape
    rows = width // (levels * PLANE)
    if rows % HEAD_DIM == 0:

        def run(ids, *refs):
            features_kernel(levels, ids, *refs)

        return call(run, ids, (grads,), [((2, tokens, levels * rows), BF16)] * 2, after)
    order = jnp.arange(levels) ^ ids[0]
    members = jnp.arange(PLANE) ^ (2 * ids[1] + ids[2])
    parts = jnp.take(grads.reshape(tokens, levels, PLANE, rows), order, axis=1)
    parts = jnp.take(parts, members, axis=2).transpose(2, 0, 1, 3)
    parts = parts.reshape(PLANE, tokens, levels * rows)
    return parts[:2], parts[2:]


def chip_rows_kernel(ids, here_ref, there_ref, *outs):
    tokens = here_ref.shape[1]
    for core, out in enumerate(outs):
        out[:tokens] = here_ref[core]
        out[tokens:] = there_ref[core]


def chip_rows(here, there, ids):
    shape = (2 * here.shape[1], here.shape[2])
    return call(chip_rows_kernel, ids, (here, there), [(shape, BF16)] * 2)


def stack_kernel(ids, *refs):
    rows = refs[0].shape[0]
    for at, ref in enumerate(refs[:-1]):
        refs[-1][at * rows : (at + 1) * rows] = ref[...]


def swap(value, distance, count):
    return lax.ppermute(value, "seq", [(i, i ^ distance) for i in range(count)])


def shift(value, r, count):
    return lax.ppermute(value, "fsdp", [(i, (i + r) % count) for i in range(count)])


def shift_across(value, r, count, devices):
    route = [
        (i * count + f, (i ^ 2) * count + (f + r) % count) for i in range(devices) for f in range(count)
    ]
    return lax.ppermute(value, ("seq", "fsdp"), route)


def chip_kernel(ids, mine_ref, pair_ref, near_ref, send_ref):
    near_ref[...] = mine_ref[0] + pair_ref[0].astype(F32)
    send_ref[...] = (mine_ref[1] + pair_ref[1].astype(F32)).astype(BF16)


def sum_kernel(ids, a_ref, b_ref, out_ref):
    out_ref[...] = (a_ref[...].astype(F32) + b_ref[...].astype(F32)).astype(BF16)


def before_kernel(reverse, ids, chip_ref, across_ref, *refs):
    near_ref, send_ref = refs[-2:]
    before = refs[0][...].astype(F32)
    for ref in refs[1:-2]:
        before = before + ref[...].astype(F32)
    second = (1 - ids[1] if reverse else ids[1]) == 1
    near_ref[...] = before + jnp.where(second, across_ref[...].astype(F32), 0.0)
    send_ref[...] = (before + jnp.where(second, 0.0, chip_ref[...])).astype(BF16)


def core_kernel(reverse, ids, near_ref, far_ref, mine_ref, pair_ref, own_ref, send_ref):
    second = (1 - ids[2] if reverse else ids[2]) == 1
    for at, ref in ((0, near_ref), (1, far_ref)):
        before = ref[...].astype(F32)
        own = before + jnp.where(second, pair_ref[at].astype(F32), 0.0)
        send = before + jnp.where(second, 0.0, mine_ref[at])
        own_ref[at] = own.astype(BF16)
        send_ref[at] = send.astype(BF16)


class Scan:
    def __init__(self, mine, send, ids, count, reverse, doubling):
        self.mine, self.ids, self.count = (mine, ids, count)
        self.reverse, self.doubling = (reverse, doubling)
        self.quarter = (SLOTS, HEAD_DIM, HEAD_DIM)
        self.pair = swap(send, 1, count)

    def chip(self, after=()):
        outs = [(self.quarter, F32), (self.quarter, BF16)]
        self.total, to_x = call(chip_kernel, self.ids, (self.mine, self.pair), outs, after)
        self.across = swap(to_x, 2, self.count)
        return self.total

    def along(self, value, step):
        move = -PLANE * step if self.reverse else PLANE * step
        route = [(i, i + move) for i in range(self.count) if 0 <= i + move < self.count]
        return lax.ppermute(value, "seq", route)

    def plane(self, after=()):
        outs = [(self.quarter, BF16)]
        (self.summed,) = call(sum_kernel, self.ids, (self.total, self.across), outs, after)
        steps = [1] if self.doubling else range(self.count // PLANE - 1, 0, -1)
        self.got = [self.along(self.summed, step) for step in steps]
        return self.summed

    def double(self, after=()):
        step = 2
        while step < self.count // PLANE:
            outs = [(self.quarter, BF16)]
            (self.summed,) = call(sum_kernel, self.ids, (self.summed, self.got[-1]), outs, after)
            self.got.append(self.along(self.summed, step))
            step *= 2
        return self.summed

    def before(self, after=()):
        def befores(ids, *refs):
            before_kernel(self.reverse, ids, *refs)

        outs = [(self.quarter, F32), (self.quarter, BF16)]
        arrays = (self.total, self.across, *self.got)
        self.near, to_x = call(befores, self.ids, arrays, outs, after)
        self.far = swap(to_x, 2, self.count)
        return self.near

    def core(self, after=()):
        def cores(ids, *refs):
            core_kernel(self.reverse, ids, *refs)

        outs = [((2, *self.quarter), BF16)] * 2
        arrays = (self.near, self.far, self.mine, self.pair)
        own, to_core = call(cores, self.ids, arrays, outs, after)
        return own, swap(to_core, 1, self.count)


def body(queries, key_vectors, value_vectors, out_grad, out_weight):
    seq_devices = lax.axis_size("seq")
    fsdp_devices = lax.axis_size("fsdp")
    batches, tokens, width = queries.shape
    rows = out_grad.shape[2] // seq_devices
    levels = seq_devices // PLANE
    piece = out_weight.shape[1]
    factor = 1.0 / math.sqrt(HEAD_DIM * tokens * seq_devices)
    grad_factor = 1.0 / math.sqrt(fsdp_devices * tokens * seq_devices)
    me = lax.axis_index("seq")
    ids = jnp.stack([me // PLANE, (me >> 1) & 1, me & 1, lax.axis_index("fsdp")]).astype(jnp.int32)
    half = (2, SLOTS, HEAD_DIM, HEAD_DIM)
    others = range(1, fsdp_devices)

    grads_own = out_grad[0]
    grads_got = [shift(grads_own, r, fsdp_devices) for r in others]
    mine, send = call(state_kernel, ids, (key_vectors, value_vectors), [(half, F32), (half, BF16)])
    s_scan = Scan(mine, send, ids, seq_devices, False, False)
    s_total = s_scan.chip()
    attn_own = dot(grads_own, out_weight, 1, 0).astype(BF16)
    here, there = features(grads_own, ids, levels, after=(s_total,))
    there = swap(there, 2, seq_devices)
    s_plane = s_scan.plane(after=(attn_own,))
    attn_got = [dot(grads, out_weight, 1, 0).astype(BF16) for grads in grads_got]
    attn_back = [shift(attn_got[r - 1], -r, fsdp_devices) for r in others]
    rows_own = chip_rows(here, there, ids)
    rows_own_other = swap(rows_own[1], 1, seq_devices)
    s_near = s_scan.before(after=(*attn_got, rows_own[0]))
    here_got, there_got = features(jnp.concatenate(grads_got), ids, levels, after=(s_near,))
    there_got = swap(there_got, 2, seq_devices)
    s_own, s_got = s_scan.core()

    def grad_states(ids, *refs):
        grad_state_kernel(fsdp_devices, ids, *refs)

    grad_attn, g_mine, g_send = call(
        grad_states,
        ids,
        (queries, attn_own, *attn_back),
        [(queries.shape, BF16), (half, F32), (half, BF16)],
        after=(s_own,),
    )

    g_scan = Scan(g_mine, g_send, ids, seq_devices, True, True)
    g_total = g_scan.chip(after=(there_got,))

    def attended_heads(ids, *refs):
        attended_kernel(fsdp_devices, factor, ids, *refs)

    attended = call(
        attended_heads,
        ids,
        (queries, key_vectors, value_vectors, s_own, s_got),
        [((tokens, piece), BF16)] * fsdp_devices,
        after=(g_total, rows_own_other),
    )
    near = [attended[0]] + [shift(attended[r], r, fsdp_devices) for r in others]
    across = [swap(attended[0], 2, seq_devices)]
    across += [shift_across(attended[r], r, fsdp_devices, seq_devices) for r in others]

    g_plane = g_scan.plane(after=attended[:1])

    def blocks(ids, *refs):
        block_kernel(factor, ids, *refs)

    flat = (tokens, width)
    query_grad, key_part, value_part, blocks_ran = call(
        blocks,
        ids,
        (queries, key_vectors, value_vectors, grad_attn, s_own, s_got),
        [(queries.shape, BF16), (flat, F32), (flat, F32), RAN],
        after=(g_plane,),
    )
    rows_got = chip_rows(here_got, there_got, ids)
    g_double = g_scan.double(after=rows_got[:1])
    g_near = g_scan.before()

    (near,) = call(
        stack_kernel,
        ids,
        (near[0], across[0], *near[1:], *across[1:]),
        [((2 * fsdp_devices * tokens, piece), BF16)],
        after=(g_double, rows_got[0]),
    )
    grads_rows = jnp.concatenate(
        [rows_own[0], rows_got[0], rows_own_other, swap(rows_got[1], 1, seq_devices)]
    )
    attended_all = jnp.concatenate([near, swap(near, 1, seq_devices)])
    partial = dot(grads_rows, attended_all, 0, 0)
    chunks = [partial[k * rows : (k + 1) * rows].astype(BF16) for k in range(levels)]
    got = [swap(chunks[k], PLANE * k, seq_devices) for k in range(1, levels)]
    g_own, g_got = g_scan.core(after=got[:2])

    def later(ids, *refs):
        later_kernel(factor, ids, *refs)

    key_grad, value_grad = call(
        later,
        ids,
        (key_vectors, value_vectors, key_part, value_part, g_own, g_got),
        [(queries.shape, BF16)] * 2,
        stored=True,
        scratch=[
            pltpu.VMEM(queries.shape, BF16),
            pltpu.VMEM(queries.shape, BF16),
            pltpu.SemaphoreType.DMA((2, SLOTS)),
        ],
    )
    weight_grad = partial[:rows]
    for chunk in got:
        weight_grad = weight_grad + chunk.astype(F32)
    return (query_grad, key_grad, value_grad, weight_grad * grad_factor)


def solution(mesh):
    in_specs = (
        P("fsdp", "seq", None),
        P("fsdp", "seq", None),
        P("fsdp", "seq", None),
        P("fsdp", "seq", None),
        P(None, "fsdp"),
    )
    out_specs = (
        P("fsdp", "seq", None),
        P("fsdp", "seq", None),
        P("fsdp", "seq", None),
        P("seq", "fsdp"),
    )
    return jax.shard_map(body, mesh=mesh, in_specs=in_specs, out_specs=out_specs, check_vma=False)
```
